32 devices in a mesh: dp: 16 (over z, y, core), tensor: 2 (over x).
Axes of the slice: x: 2, y: 2, z: 4, core: 2. Of those that a mesh axis runs over, the one named last changes fastest.
Arguments:
- train_hidden: bfloat16 [16, 128, 28672], P('dp', None, 'tensor'), may hold values from -6 to 6
- train_grad: bfloat16 [16, 128, 8192], P('dp', None, 'tensor'), may hold values from -6 to 6
- test_hidden: bfloat16 [16, 64, 28672], P('dp', None, 'tensor'), may hold values from -6 to 6
- test_grad: bfloat16 [16, 64, 8192], P('dp', None, 'tensor'), may hold values from -6 to 6
- proj_in: bfloat16 [64, 28672], P(None, 'tensor'), may hold values from -0.03125 to 0.03125
- proj_out: bfloat16 [64, 8192], P(None, 'tensor'), may hold values from -0.0625 to 0.0625
- precond_in: float32 [64, 64], replicated, may hold values from -0.75 to 0.75
- precond_out: float32 [64, 64], replicated, may hold values from -0.75 to 0.75
Outputs:
- scores: float32 [16, 16], P('dp', 'tensor')
The draws below stay inside these ranges and needn't reach their ends.
All inputs are finite; a program needn't handle non-finite values.
Results may differ from the reference program's by a relative error of at most 0.0029.
Values may be sent and summed in bfloat16 or wider, within the bound.
A program may use at most 64 MiB of HBM per device.

```python
import math
import jax
import jax.numpy as jnp
from jax import lax

D = 8192
FF = 28672
RANK = 64
SEQ = 128
QRY_TOK = 64
EXAMPLES = 16
QUERIES = 16


def steps_of(rng, extent, pieces, low, top_value):
    level, own = 1.0, jax.random.fold_in(rng, 6)
    for dim, shards_of in pieces:
        heights = jnp.exp(jax.random.uniform(jax.random.fold_in(own, dim), (shards_of,), jnp.float32, low / len(pieces), top_value / len(pieces)))
        level = level * jnp.repeat(heights, extent[dim] // shards_of).reshape([-1 if axis == dim else 1 for axis in range(len(extent))])
    return level


def centred(own_key, dims, deviation, bound, pieces=(), dtype=jnp.bfloat16):
    gain = steps_of(own_key, dims, pieces, -0.22, 0.18) if pieces else 1.0
    entries = jax.random.normal(own_key, dims, jnp.float32) * deviation * gain
    return jnp.minimum(jnp.maximum(entries, -bound), bound).astype(dtype)


def setup_inputs(seed: int = 0) -> dict:
    key_list = jax.random.split(jax.random.key(seed), 9)
    return {
        "train_hidden": centred(key_list[0], (EXAMPLES, SEQ, FF), 1.0, 6.0, ((0, 16), (2, 2))),
        "train_grad": centred(key_list[1], (EXAMPLES, SEQ, D), 1.0, 6.0, ((0, 16), (2, 2))),
        "test_hidden": centred(key_list[2], (QUERIES, QRY_TOK, FF), 1.0, 6.0, ((0, 16), (2, 2))),
        "test_grad": centred(key_list[3], (QUERIES, QRY_TOK, D), 1.0, 6.0, ((0, 16), (2, 2))),
        "proj_in": centred(key_list[4], (RANK, FF), FF ** -0.5, 0.03125, ((1, 2),)),
        "proj_out": centred(key_list[5], (RANK, D), D ** -0.5, 0.0625, ((1, 2),)),
        "precond_in": centred(key_list[6], (RANK, RANK), RANK ** -0.5, 0.75, (), jnp.float32),
        "precond_out": centred(key_list[7], (RANK, RANK), RANK ** -0.5, 0.75, (), jnp.float32),
    }


def make_sketch(hidden, grad, proj_in, proj_out):
    left = jnp.dot(hidden, proj_in.T, preferred_element_type=jnp.float32)
    right = jnp.dot(grad, proj_out.T, preferred_element_type=jnp.float32)
    return jnp.dot(left.T, right, precision=lax.Precision.HIGHEST, preferred_element_type=jnp.float32)

def reference(train_hidden, train_grad, test_hidden, test_grad, proj_in, proj_out, precond_in, precond_out):

    def train_one(pair):
        return make_sketch(pair[0], pair[1], proj_in, proj_out)
    train_sketch = lax.map(train_one, (train_hidden, train_grad))
    test_sketch = lax.map(train_one, (test_hidden, test_grad))
    halfway = jnp.einsum('ai,qij->qaj', precond_in, test_sketch, precision=lax.Precision.HIGHEST)
    conditioned = jnp.einsum('qaj,jb->qab', halfway, precond_out, precision=lax.Precision.HIGHEST)
    conditioned = conditioned.astype(jnp.bfloat16)
    factor = 1.0 / (RANK * math.sqrt(SEQ * QRY_TOK))
    scores = jnp.einsum('eab,qab->eq', train_sketch, conditioned.astype(jnp.float32), precision=lax.Precision.HIGHEST)
    return scores * factor
```

```python
import functools
import math

import jax
import jax.numpy as jnp
from jax import lax
from jax.experimental import pallas as pl
from jax.experimental.pallas import tpu as pltpu
from jax.sharding import PartitionSpec as P

MESH = pl.DeviceIdType.MESH
EXACT = lax.Precision.HIGHEST


def each(low, high, step):
    if high - low <= 16:
        for k in range(low, high):
            step(k)
    else:
        lax.fori_loop(low, high, lambda k, _: (step(k), 0)[1], 0)


def project(rows, factor):
    return lax.dot_general(
        rows, factor, (((1,), (1,)), ((), ())), preferred_element_type=jnp.float32
    )


def outer_sum(left, right):
    return lax.dot_general(
        left, right, (((0,), (0,)), ((), ())), precision=EXACT, preferred_element_type=jnp.float32
    )


def times(a, b):
    return jnp.dot(a, b, precision=EXACT, preferred_element_type=jnp.float32)


def side_by_side(rows, fold):
    height = rows.shape[0] // fold
    return jnp.concatenate([rows[i * height : (i + 1) * height] for i in range(fold)], axis=1)


def one_above_other(rows, fold):
    width = rows.shape[1] // fold
    return jnp.concatenate([rows[:, i * width : (i + 1) * width] for i in range(fold)], axis=0)


def kernel(
    n_dp, n_tensor, chunks, fold, factor,
    th_hbm, tg_hbm, qh_hbm, qg_hbm, pi_hbm, po_hbm, ci_hbm, co_hbm,
    out_ref,
    th, tg, qh, qg, pi, po, ci, co,
    rq_own, rq_in, rt_own, rt_in, c_own, c_in, t_own, t_in, gathered, part, part_in,
    load_sem, pi_sem, qh_sem, th_sem,
    rq_send, rq_recv, rt_send, rt_recv, c_send, c_recv, t_send, t_recv,
    g_send, g_recv, p_send, p_recv,
):
    me_dp = lax.axis_index("dp")
    me_t = lax.axis_index("tensor")
    hid = pi.shape[1]
    step = hid // chunks

    def load(src, dst, sem):
        return pltpu.make_async_copy(src, dst, sem)

    def piece(c):
        return pl.ds(pl.multiple_of(c * step, step), step)

    po_load = load(po_hbm, po, load_sem.at[0])
    qg_load = load(qg_hbm, qg, load_sem.at[1])
    tg_load = load(tg_hbm, tg, load_sem.at[2])
    ci_load = load(ci_hbm, ci, load_sem.at[3])
    co_load = load(co_hbm, co, load_sem.at[4])
    pi_load = lambda c: load(pi_hbm.at[:, piece(c)], pi.at[:, piece(c)], pi_sem.at[c])
    qh_load = lambda c: load(qh_hbm.at[:, :, piece(c)], qh.at[:, :, piece(c)], qh_sem.at[c])
    th_load = lambda c: load(th_hbm.at[:, :, piece(c)], th.at[:, :, piece(c)], th_sem.at[c])

    po_load.start()
    qg_load.start()
    co_load.start()
    ci_load.start()
    for c in range(chunks):
        pi_load(c).start()
        qh_load(c).start()
    tg_load.start()
    for c in range(chunks):
        th_load(c).start()

    barrier = pltpu.get_barrier_semaphore()

    def greet_tensor(k):
        peer = lax.rem(me_t + k, n_tensor)
        pl.semaphore_signal(barrier, inc=1, device_id={"tensor": peer}, device_id_type=MESH)

    def greet_dp(k):
        peer = lax.rem(me_dp + k, n_dp)
        pl.semaphore_signal(barrier, inc=1, device_id={"dp": peer}, device_id_type=MESH)

    each(1, n_tensor, greet_tensor)
    each(1, n_dp, greet_dp)

    def swap(own, landing, send, recv, k, shared):
        peer = lax.rem(me_t + k, n_tensor)
        return pltpu.make_async_remote_copy(
            src_ref=own if shared else own.at[peer],
            dst_ref=landing.at[k - 1],
            send_sem=send.at[k - 1],
            recv_sem=recv.at[k - 1],
            device_id={"tensor": peer},
            device_id_type=MESH,
        )

    rq_swap = lambda k: swap(rq_own, rq_in, rq_send, rq_recv, k, True)
    rt_swap = lambda k: swap(rt_own, rt_in, rt_send, rt_recv, k, True)
    c_swap = lambda k: swap(c_own, c_in, c_send, c_recv, k, False)
    t_swap = lambda k: swap(t_own, t_in, t_send, t_recv, k, False)

    def spread(k):
        return pltpu.make_async_remote_copy(
            src_ref=gathered.at[me_dp],
            dst_ref=gathered.at[me_dp],
            send_sem=g_send.at[k - 1],
            recv_sem=g_recv.at[k - 1],
            device_id={"dp": lax.rem(me_dp + k, n_dp)},
            device_id_type=MESH,
        )

    def summed(own, landing, one_swap):
        total = own
        for k in range(1, n_tensor):
            one_swap(k).wait_recv()
            total = total + landing[k - 1]
        return total

    def put_shares(dst, whole):
        rows = whole.shape[0] // n_tensor
        for t in range(n_tensor):
            dst[t] = side_by_side(whole[t * rows : (t + 1) * rows], fold)

    po_load.wait()
    qg_load.wait()
    rq_own[...] = side_by_side(project(qg[0], po[...]), 2)
    pl.semaphore_wait(barrier, n_dp + n_tensor - 2)
    for k in range(1, n_tensor):
        rq_swap(k).start()

    def query_chunk(c, total):
        pi_load(c).wait()
        qh_load(c).wait()
        return total + project(qh[0, :, piece(c)], pi[:, piece(c)])

    left = lax.fori_loop(0, chunks, query_chunk, jnp.zeros((qh.shape[1], pi.shape[0]), jnp.float32))
    ci_load.wait()
    co_load.wait()
    right = one_above_other(summed(rq_own[...], rq_in, rq_swap), 2)
    put_shares(c_own, times(ci[...], outer_sum(left, times(right, co[...]))))
    for k in range(1, n_tensor):
        c_swap(k).start()

    tg_load.wait()
    rt_own[...] = side_by_side(project(tg[0], po[...]), 2)
    for k in range(1, n_tensor):
        rt_swap(k).start()

    def example_chunk(c, total):
        th_load(c).wait()
        return total + project(th[0, :, piece(c)], pi[:, piece(c)])

    left = lax.fori_loop(
        0, chunks, example_chunk, jnp.zeros((th.shape[1], pi.shape[0]), jnp.float32)
    )

    gathered[me_dp] = summed(c_own[me_t], c_in, c_swap).astype(gathered.dtype)
    each(1, n_dp, lambda k: spread(k).start())

    right = one_above_other(summed(rt_own[...], rt_in, rt_swap), 2)
    put_shares(t_own, outer_sum(left, right))
    for k in range(1, n_tensor):
        t_swap(k).start()
    share = summed(t_own[me_t], t_in, t_swap)

    each(1, n_dp, lambda k: spread(k).wait_recv())
    lanes = jnp.sum(gathered[...].astype(jnp.float32) * share[None], axis=1)
    part[...] = lanes.reshape(part.shape)
    p_swap = lambda k: swap(part, part_in, p_send, p_recv, k, False)
    for k in range(1, n_tensor):
        p_swap(k).start()
    total = summed(part[me_t], part_in, p_swap)
    out_ref[...] = jnp.sum(total.T, axis=0, keepdims=True) * factor

    for one_swap in (rq_swap, rt_swap, c_swap, t_swap, p_swap):
        for k in range(1, n_tensor):
            one_swap(k).wait_send()
    each(1, n_dp, lambda k: spread(k).wait_send())


def shards(n_dp, n_tensor, th, tg, qh, qg, pi, po, ci, co):
    rank, hid = pi.shape
    seq, qry = th.shape[1], qh.shape[1]
    share = rank // n_tensor
    fold = 2 if share % 32 == 0 else 1
    packed = (share // fold, rank * fold)
    kept = n_dp // n_tensor
    chunks = 7
    f32, bf16 = jnp.float32, jnp.bfloat16
    dma = pltpu.SemaphoreType.DMA
    others = n_tensor - 1
    factor = 1.0 / (rank * math.sqrt(seq * qry))
    args = (th, tg, qh, qg, pi, po, ci, co)
    pair = dma((others,))
    rows = (seq + qry) * rank * 2
    return pl.pallas_call(
        functools.partial(kernel, n_dp, n_tensor, chunks, fold, factor),
        out_shape=jax.ShapeDtypeStruct((1, kept), f32),
        in_specs=[pl.BlockSpec(memory_space=pl.ANY)] * len(args),
        out_specs=pl.BlockSpec(memory_space=pltpu.VMEM),
        scratch_shapes=[pltpu.VMEM(a.shape, a.dtype) for a in args]
        + [
            pltpu.VMEM((qry // 2, 2 * rank), f32),
            pltpu.VMEM((others, qry // 2, 2 * rank), f32),
            pltpu.VMEM((seq // 2, 2 * rank), f32),
            pltpu.VMEM((others, seq // 2, 2 * rank), f32),
            pltpu.VMEM((n_tensor,) + packed, f32),
            pltpu.VMEM((others,) + packed, f32),
            pltpu.VMEM((n_tensor,) + packed, f32),
            pltpu.VMEM((others,) + packed, f32),
            pltpu.VMEM((n_dp,) + packed, bf16),
            pltpu.VMEM((n_tensor, kept, packed[1]), f32),
            pltpu.VMEM((others, kept, packed[1]), f32),
            dma((5,)), dma((chunks,)), dma((chunks,)), dma((chunks,)),
        ]
        + [pair] * 8
        + [dma((n_dp - 1,)), dma((n_dp - 1,)), pair, pair],
        cost_estimate=pl.CostEstimate(
            flops=rows * (hid + po.shape[1]),
            bytes_accessed=sum(a.size * a.dtype.itemsize for a in args),
            transcendentals=0,
        ),
        compiler_params=pltpu.CompilerParams(
            collective_id=0, has_side_effects=True, vmem_limit_bytes=48 * 1024 * 1024
        ),
    )(*args)


def solution(mesh):
    placed = (
        P("dp", None, "tensor"),
        P("dp", None, "tensor"),
        P("dp", None, "tensor"),
        P("dp", None, "tensor"),
        P(None, "tensor"),
        P(None, "tensor"),
        P(),
        P(),
    )
    body = functools.partial(shards, mesh.shape["dp"], mesh.shape["tensor"])
    return jax.shard_map(
        body, mesh=mesh, in_specs=placed, out_specs=P("dp", "tensor"), check_vma=False
    )
```

```python
import functools
import math

import jax
import jax.numpy as jnp
from jax import lax
from jax.experimental import pallas as pl
from jax.experimental.pallas import tpu as pltpu
from jax.sharding import PartitionSpec as P

MESH = pl.DeviceIdType.MESH


def each(low, high, step):
    if high - low <= 16:
        for k in range(low, high):
            step(k)
    else:
        lax.fori_loop(low, high, lambda k, _: (step(k), 0)[1], 0)


def project(rows, factor):
    return lax.dot_general(
        rows, factor, (((1,), (1,)), ((), ())), preferred_element_type=jnp.float32
    )


def hi_lo(x):
    hi = x.astype(jnp.bfloat16)
    return hi, (x - hi.astype(jnp.float32)).astype(jnp.bfloat16)


def hi_beside_lo(twins):
    hi, lo = hi_lo(twins)
    lane = lax.broadcasted_iota(jnp.int32, twins.shape, 1)
    return jnp.where(lane < twins.shape[1] // 2, hi.astype(jnp.float32), lo.astype(jnp.float32)).astype(
        jnp.bfloat16
    )


def twins(x):
    return jnp.concatenate([x, x], axis=1)


def fold_twins(y):
    width = y.shape[1] // 2
    while width > 64:
        y = y[:, :width] + y[:, width:]
        width //= 2
    return y + jnp.concatenate([y[:, width:], y[:, :width]], axis=1)


def dot(a, b):
    return jnp.dot(a, b, preferred_element_type=jnp.float32)


def split_dot(a, parts):
    both = jnp.concatenate(hi_lo(a), axis=0)
    y = dot(both, parts)
    return y[: a.shape[0]] + y[a.shape[0] :]


def kernel(
    n_dp, n_tensor, chunks, fold, factor,
    th_hbm, tg_hbm, qh_hbm, qg_hbm, pi_hbm, po_hbm, ci_hbm, co_hbm,
    out_ref,
    th, tg, qh, qg, pi, po, ci, co,
    rq_own, rq_in, rt_own, rt_in, c_own, c_in, t_own, t_in, gathered, part, part_in,
    load_sem, pi_sem, qh_sem, th_sem,
    rq_send, rq_recv, rt_send, rt_recv, c_send, c_recv, t_send, t_recv,
    g_send, g_recv, p_send, p_recv,
):
    me_dp = lax.axis_index("dp")
    me_t = lax.axis_index("tensor")
    hid = pi.shape[1]
    step = hid // chunks

    def load(src, dst, sem):
        return pltpu.make_async_copy(src, dst, sem)

    def piece(c):
        return pl.ds(pl.multiple_of(c * step, step), step)

    po_load = load(po_hbm, po, load_sem.at[0])
    qg_load = load(qg_hbm, qg, load_sem.at[1])
    tg_load = load(tg_hbm, tg, load_sem.at[2])
    ci_load = load(ci_hbm, ci, load_sem.at[3])
    co_load = load(co_hbm, co, load_sem.at[4])
    pi_load = lambda c: load(pi_hbm.at[:, piece(c)], pi.at[:, piece(c)], pi_sem.at[c])
    qh_load = lambda c: load(qh_hbm.at[:, :, piece(c)], qh.at[:, :, piece(c)], qh_sem.at[c])
    th_load = lambda c: load(th_hbm.at[:, :, piece(c)], th.at[:, :, piece(c)], th_sem.at[c])

    po_load.start()
    qg_load.start()

    barrier = pltpu.get_barrier_semaphore()

    def greet_tensor(k):
        peer = lax.rem(me_t + k, n_tensor)
        pl.semaphore_signal(barrier, inc=1, device_id={"tensor": peer}, device_id_type=MESH)

    def greet_dp(k):
        peer = lax.rem(me_dp + k, n_dp)
        pl.semaphore_signal(barrier, inc=1, device_id={"dp": peer}, device_id_type=MESH)

    for c in range(chunks):
        pi_load(c).start()
        qh_load(c).start()
    co_load.start()
    ci_load.start()
    each(1, n_tensor, greet_tensor)
    each(1, n_dp, greet_dp)
    tg_load.start()
    for c in range(chunks):
        th_load(c).start()

    def swap(own, landing, send, recv, k, shared):
        peer = lax.rem(me_t + k, n_tensor)
        return pltpu.make_async_remote_copy(
            src_ref=own if shared else own.at[peer],
            dst_ref=landing.at[k - 1],
            send_sem=send.at[k - 1],
            recv_sem=recv.at[k - 1],
            device_id={"tensor": peer},
            device_id_type=MESH,
        )

    rq_swap = lambda k: swap(rq_own, rq_in, rq_send, rq_recv, k, True)
    rt_swap = lambda k: swap(rt_own, rt_in, rt_send, rt_recv, k, True)
    c_swap = lambda k: swap(c_own, c_in, c_send, c_recv, k, False)
    t_swap = lambda k: swap(t_own, t_in, t_send, t_recv, k, False)

    def spread(k):
        return pltpu.make_async_remote_copy(
            src_ref=gathered.at[me_dp],
            dst_ref=gathered.at[me_dp],
            send_sem=g_send.at[k - 1],
            recv_sem=g_recv.at[k - 1],
            device_id={"dp": lax.rem(me_dp + k, n_dp)},
            device_id_type=MESH,
        )

    def summed(own, landing, one_swap):
        total = own
        for k in range(1, n_tensor):
            one_swap(k).wait_recv()
            total = total + landing[k - 1]
        return total

    def put_shares(dst, whole):
        rows = whole.shape[0] // n_tensor
        for t in range(n_tensor):
            own = whole[t * rows : (t + 1) * rows]
            if fold == 2:
                lane = lax.broadcasted_iota(jnp.int32, (rows // 2, own.shape[1]), 1)
                dst[t] = jnp.where(lane < own.shape[1] // 2, own[: rows // 2], own[rows // 2 :])
            else:
                dst[t] = own[:, : own.shape[1] // 2]

    po_load.wait()
    qg_load.wait()
    rq_own[...] = hi_beside_lo(twins(project(qg[0], po[...])))
    pl.semaphore_wait(barrier, n_dp + n_tensor - 2)
    for k in range(1, n_tensor):
        rq_swap(k).start()

    def query_chunk(c, total):
        pi_load(c).wait()
        qh_load(c).wait()
        return total + project(pi[:, piece(c)], qh[0, :, piece(c)])

    left = lax.fori_loop(
        0, chunks - 1, query_chunk, jnp.zeros((pi.shape[0], qh.shape[1]), jnp.float32)
    )
    ci_load.wait()
    co_load.wait()
    co_parts = hi_beside_lo(twins(co[...]))
    co_parts = jnp.concatenate([co_parts, co_parts], axis=0)
    ci_parts = jnp.concatenate(hi_lo(ci[...]), axis=0)
    right = dot(rq_own[...], co_parts)
    for k in range(1, n_tensor):
        rq_swap(k).wait_recv()
        right = right + dot(rq_in[k - 1], co_parts)
    right = hi_beside_lo(fold_twins(right))
    left = query_chunk(chunks - 1, left)
    sketch = split_dot(left, right)
    halves = dot(ci_parts, jnp.concatenate(hi_lo(sketch), axis=1))
    rank = ci.shape[0]
    put_shares(c_own, fold_twins(halves[:rank] + halves[rank:]))
    for k in range(1, n_tensor):
        c_swap(k).start()

    tg_load.wait()
    rt_own[...] = hi_beside_lo(twins(project(tg[0], po[...])))
    for k in range(1, n_tensor):
        rt_swap(k).start()

    def example_chunk(c, total):
        th_load(c).wait()
        return total + project(pi[:, piece(c)], th[0, :, piece(c)])

    left = lax.fori_loop(
        0, chunks, example_chunk, jnp.zeros((pi.shape[0], th.shape[1]), jnp.float32)
    )

    gathered[me_dp] = summed(c_own[me_t], c_in, c_swap).astype(gathered.dtype)
    each(1, n_dp, lambda k: spread(k).start())

    rights = [rt_own[...]]
    for k in range(1, n_tensor):
        rt_swap(k).wait_recv()
        rights.append(rt_in[k - 1])
    put_shares(t_own, fold_twins(split_dot(left, jnp.concatenate(rights, axis=1))))
    for k in range(1, n_tensor):
        t_swap(k).start()
    share = summed(t_own[me_t], t_in, t_swap)

    each(1, n_dp, lambda k: spread(k).wait_recv())
    lanes = jnp.sum(gathered[...].astype(jnp.float32) * share[None], axis=1)
    part[...] = lanes.reshape(part.shape)
    p_swap = lambda k: swap(part, part_in, p_send, p_recv, k, False)
    for k in range(1, n_tensor):
        p_swap(k).start()
    total = summed(part[me_t], part_in, p_swap)
    out_ref[...] = jnp.sum(total.T, axis=0, keepdims=True) * factor

    for one_swap in (rq_swap, rt_swap, c_swap, t_swap, p_swap):
        for k in range(1, n_tensor):
            one_swap(k).wait_send()
    each(1, n_dp, lambda k: spread(k).wait_send())


def shards(n_dp, n_tensor, th, tg, qh, qg, pi, po, ci, co):
    rank, hid = pi.shape
    seq, qry = th.shape[1], qh.shape[1]
    share = rank // n_tensor
    fold = 2 if share % 32 == 0 else 1
    packed = (share // fold, rank * fold)
    kept = n_dp // n_tensor
    chunks = 7
    f32, bf16 = jnp.float32, jnp.bfloat16
    dma = pltpu.SemaphoreType.DMA
    others = n_tensor - 1
    factor = 1.0 / (rank * math.sqrt(seq * qry))
    args = (th, tg, qh, qg, pi, po, ci, co)
    pair = dma((others,))
    rows = (seq + qry) * rank * 2
    return pl.pallas_call(
        functools.partial(kernel, n_dp, n_tensor, chunks, fold, factor),
        out_shape=jax.ShapeDtypeStruct((1, kept), f32),
        in_specs=[pl.BlockSpec(memory_space=pltpu.HBM)] * len(args),
        out_specs=pl.BlockSpec(memory_space=pltpu.VMEM),
        scratch_shapes=[pltpu.VMEM(a.shape, a.dtype) for a in args]
        + [
            pltpu.VMEM((qry, 2 * rank), bf16),
            pltpu.VMEM((others, qry, 2 * rank), bf16),
            pltpu.VMEM((seq, 2 * rank), bf16),
            pltpu.VMEM((others, seq, 2 * rank), bf16),
            pltpu.VMEM((n_tensor,) + packed, f32),
            pltpu.VMEM((others,) + packed, f32),
            pltpu.VMEM((n_tensor,) + packed, f32),
            pltpu.VMEM((others,) + packed, f32),
            pltpu.VMEM((n_dp,) + packed, bf16),
            pltpu.VMEM((n_tensor, kept, packed[1]), f32),
            pltpu.VMEM((others, kept, packed[1]), f32),
            dma((5,)), dma((chunks,)), dma((chunks,)), dma((chunks,)),
        ]
        + [pair] * 8
        + [dma((n_dp - 1,)), dma((n_dp - 1,)), pair, pair],
        cost_estimate=pl.CostEstimate(
            flops=rows * (hid + po.shape[1]),
            bytes_accessed=sum(a.size * a.dtype.itemsize for a in args),
            transcendentals=0,
        ),
        compiler_params=pltpu.CompilerParams(
            collective_id=0, has_side_effects=True, vmem_limit_bytes=60 * 1024 * 1024
        ),
    )(*args)


def solution(mesh):
    placed = (
        P("dp", None, "tensor"),
        P("dp", None, "tensor"),
        P("dp", None, "tensor"),
        P("dp", None, "tensor"),
        P(None, "tensor"),
        P(None, "tensor"),
        P(),
        P(),
    )
    body = functools.partial(shards, mesh.shape["dp"], mesh.shape["tensor"])
    return jax.shard_map(
        body, mesh=mesh, in_specs=placed, out_specs=P("dp", "tensor"), check_vma=False
    )
```

```python
import functools
import math

import jax
import jax.numpy as jnp
from jax import lax
from jax.experimental import pallas as pl
from jax.experimental.pallas import tpu as pltpu
from jax.sharding import PartitionSpec as P

MESH = pl.DeviceIdType.MESH


def each(low, high, step):
    if high - low <= 16:
        for k in range(low, high):
            step(k)
    else:
        lax.fori_loop(low, high, lambda k, _: (step(k), 0)[1], 0)


def project(rows, factor):
    return lax.dot_general(
        rows, factor, (((1,), (1,)), ((), ())), preferred_element_type=jnp.float32
    )


def hi_lo(x):
    hi = x.astype(jnp.bfloat16)
    return hi, (x - hi.astype(jnp.float32)).astype(jnp.bfloat16)


def hi_beside_lo(twins):
    hi, lo = hi_lo(twins)
    lane = lax.broadcasted_iota(jnp.int32, twins.shape, 1)
    return jnp.where(lane < twins.shape[1] // 2, hi.astype(jnp.float32), lo.astype(jnp.float32)).astype(
        jnp.bfloat16
    )


def twins(x):
    return jnp.concatenate([x, x], axis=1)


def fold_twins(y):
    width = y.shape[1] // 2
    while width > 64:
        y = y[:, :width] + y[:, width:]
        width //= 2
    return y + jnp.concatenate([y[:, width:], y[:, :width]], axis=1)


def dot(a, b):
    return jnp.dot(a, b, preferred_element_type=jnp.float32)


def fold_rows(y):
    height = y.shape[0] // 2
    return y[:height] + y[height:]


def pack(own, fold):
    rows, lanes = own.shape
    if fold == 1:
        return own[:, : lanes // 2]
    lane = lax.broadcasted_iota(jnp.int32, (rows // 2, lanes), 1)
    return jnp.where(lane < lanes // 2, own[: rows // 2], own[rows // 2 :])


def kernel(
    n_dp, n_tensor, chunks, fold, factor,
    th_hbm, tg_hbm, qh_hbm, qg_hbm, pi_hbm, po_hbm, ci_hbm, co_hbm,
    out_ref,
    th, tg, qh, qg, pi, po, ci, co,
    rq_own, rq_in, rt_own, rt_in, lq_own, lq_in, lt_own, lt_in, gathered, part, part_in,
    load_sem, pi_sem, qh_sem, th_sem,
    rq_send, rq_recv, rt_send, rt_recv, lq_send, lq_recv, lt_send, lt_recv,
    g_send, g_recv, p_send, p_recv,
):
    me_dp = lax.axis_index("dp")
    me_t = lax.axis_index("tensor")
    hid = pi.shape[1]
    step = hid // chunks

    def load(src, dst, sem):
        return pltpu.make_async_copy(src, dst, sem)

    def piece(c):
        return pl.ds(pl.multiple_of(c * step, step), step)

    po_load = load(po_hbm, po, load_sem.at[0])
    qg_load = load(qg_hbm, qg, load_sem.at[1])
    tg_load = load(tg_hbm, tg, load_sem.at[2])
    ci_load = load(ci_hbm, ci, load_sem.at[3])
    co_load = load(co_hbm, co, load_sem.at[4])
    pi_load = lambda c: load(pi_hbm.at[:, piece(c)], pi.at[:, piece(c)], pi_sem.at[c])
    qh_load = lambda c: load(qh_hbm.at[:, :, piece(c)], qh.at[:, :, piece(c)], qh_sem.at[c])
    th_load = lambda c: load(th_hbm.at[:, :, piece(c)], th.at[:, :, piece(c)], th_sem.at[c])

    po_load.start()
    qg_load.start()

    barrier = pltpu.get_barrier_semaphore()

    def greet_tensor(k):
        peer = lax.rem(me_t + k, n_tensor)
        pl.semaphore_signal(barrier, inc=1, device_id={"tensor": peer}, device_id_type=MESH)

    def greet_dp(k):
        peer = lax.rem(me_dp + k, n_dp)
        pl.semaphore_signal(barrier, inc=1, device_id={"dp": peer}, device_id_type=MESH)

    for c in range(chunks):
        pi_load(c).start()
        qh_load(c).start()
    co_load.start()
    ci_load.start()
    each(1, n_tensor, greet_tensor)
    each(1, n_dp, greet_dp)
    def swap(own, landing, send, recv, k, shared):
        peer = lax.rem(me_t + k, n_tensor)
        return pltpu.make_async_remote_copy(
            src_ref=own if shared else own.at[peer],
            dst_ref=landing.at[k - 1],
            send_sem=send.at[k - 1],
            recv_sem=recv.at[k - 1],
            device_id={"tensor": peer},
            device_id_type=MESH,
        )

    rq_swap = lambda k: swap(rq_own, rq_in, rq_send, rq_recv, k, True)
    rt_swap = lambda k: swap(rt_own, rt_in, rt_send, rt_recv, k, True)
    lq_swap = lambda k: swap(lq_own, lq_in, lq_send, lq_recv, k, False)
    lt_swap = lambda k: swap(lt_own, lt_in, lt_send, lt_recv, k, False)

    def spread(k):
        return pltpu.make_async_remote_copy(
            src_ref=gathered.at[me_dp],
            dst_ref=gathered.at[me_dp],
            send_sem=g_send.at[k - 1],
            recv_sem=g_recv.at[k - 1],
            device_id={"dp": lax.rem(me_dp + k, n_dp)},
            device_id_type=MESH,
        )

    def summed(own, landing, one_swap):
        total = own
        for k in range(1, n_tensor):
            one_swap(k).wait_recv()
            total = total + landing[k - 1]
        return total

    rank = ci.shape[0]
    rows = rank // n_tensor

    po_load.wait()
    qg_load.wait()
    tg_load.start()
    rq_own[...] = hi_beside_lo(twins(project(qg[0], po[...])))
    pl.semaphore_wait(barrier, n_dp + n_tensor - 2)
    for k in range(1, n_tensor):
        rq_swap(k).start()

    def query_chunk(c, total):
        pi_load(c).wait()
        qh_load(c).wait()
        th_load(c).start()
        return total + project(pi[:, piece(c)], qh[0, :, piece(c)])

    left = lax.fori_loop(
        0, chunks, query_chunk, jnp.zeros((rank, qh.shape[1]), jnp.float32)
    )
    ci_load.wait()
    ci_parts = jnp.concatenate(hi_lo(ci[...]), axis=0)
    left = fold_rows(dot(ci_parts, hi_beside_lo(twins(left))))
    left = hi_beside_lo(fold_twins(left))
    for t in range(n_tensor):
        lq_own[t] = left[t * rows : (t + 1) * rows]
    for k in range(1, n_tensor):
        lq_swap(k).start()

    tg_load.wait()
    rt_own[...] = hi_beside_lo(twins(project(tg[0], po[...])))
    for k in range(1, n_tensor):
        rt_swap(k).start()

    co_load.wait()
    co_parts = hi_beside_lo(twins(co[...]))
    co_parts = jnp.concatenate([co_parts, co_parts], axis=0)
    right = dot(rq_own[...], co_parts)
    for k in range(1, n_tensor):
        rq_swap(k).wait_recv()
        right = right + dot(rq_in[k - 1], co_parts)
    right = hi_beside_lo(fold_twins(right))
    right = jnp.concatenate([right] * (2 * n_tensor), axis=0)

    def example_chunk(c, total):
        th_load(c).wait()
        return total + project(pi[:, piece(c)], th[0, :, piece(c)])

    before = chunks // 2
    example = lax.fori_loop(
        0, before, example_chunk, jnp.zeros((rank, th.shape[1]), jnp.float32)
    )

    lefts = [lq_own[me_t]]
    for k in range(1, n_tensor):
        lq_swap(k).wait_recv()
        lefts.append(lq_in[k - 1])
    conditioned = fold_twins(dot(jnp.concatenate(lefts, axis=1), right))
    gathered[me_dp] = pack(conditioned, fold).astype(gathered.dtype)
    each(1, n_dp, lambda k: spread(k).start())

    example = lax.fori_loop(before, chunks, example_chunk, example)
    for t in range(n_tensor):
        lt_own[t] = example[t * rows : (t + 1) * rows]
    for k in range(1, n_tensor):
        lt_swap(k).start()

    rights = [rt_own[...]]
    for k in range(1, n_tensor):
        rt_swap(k).wait_recv()
        rights.append(rt_in[k - 1])
    rights = jnp.concatenate(rights, axis=1)
    mine = jnp.concatenate(hi_lo(summed(lt_own[me_t], lt_in, lt_swap)), axis=0)
    share = pack(fold_twins(fold_rows(dot(mine, rights))), fold)

    each(1, n_dp, lambda k: spread(k).wait_recv())
    lanes = jnp.sum(gathered[...].astype(jnp.float32) * share[None], axis=1)
    part[...] = lanes.reshape(part.shape)
    p_swap = lambda k: swap(part, part_in, p_send, p_recv, k, False)
    for k in range(1, n_tensor):
        p_swap(k).start()
    total = summed(part[me_t], part_in, p_swap)
    out_ref[...] = jnp.sum(total.T, axis=0, keepdims=True) * factor

    for one_swap in (rq_swap, rt_swap, lq_swap, lt_swap, p_swap):
        for k in range(1, n_tensor):
            one_swap(k).wait_send()
    each(1, n_dp, lambda k: spread(k).wait_send())


def shards(n_dp, n_tensor, th, tg, qh, qg, pi, po, ci, co):
    rank, hid = pi.shape
    seq, qry = th.shape[1], qh.shape[1]
    share = rank // n_tensor
    fold = 2 if share % 32 == 0 else 1
    packed = (share // fold, rank * fold)
    kept = n_dp // n_tensor
    chunks = 7
    f32, bf16 = jnp.float32, jnp.bfloat16
    dma = pltpu.SemaphoreType.DMA
    others = n_tensor - 1
    factor = 1.0 / (rank * math.sqrt(seq * qry))
    args = (th, tg, qh, qg, pi, po, ci, co)
    pair = dma((others,))
    rows = (seq + qry) * rank * 2
    return pl.pallas_call(
        functools.partial(kernel, n_dp, n_tensor, chunks, fold, factor),
        out_shape=jax.ShapeDtypeStruct((1, kept), f32),
        in_specs=[pl.BlockSpec(memory_space=pltpu.HBM)] * len(args),
        out_specs=pl.BlockSpec(memory_space=pltpu.VMEM),
        scratch_shapes=[pltpu.VMEM(a.shape, a.dtype) for a in args]
        + [
            pltpu.VMEM((qry, 2 * rank), bf16),
            pltpu.VMEM((others, qry, 2 * rank), bf16),
            pltpu.VMEM((seq, 2 * rank), bf16),
            pltpu.VMEM((others, seq, 2 * rank), bf16),
            pltpu.VMEM((n_tensor, share, 2 * rank), bf16),
            pltpu.VMEM((others, share, 2 * rank), bf16),
            pltpu.VMEM((n_tensor, share, seq), f32),
            pltpu.VMEM((others, share, seq), f32),
            pltpu.VMEM((n_dp,) + packed, bf16),
            pltpu.VMEM((n_tensor, kept, packed[1]), f32),
            pltpu.VMEM((others, kept, packed[1]), f32),
            dma((5,)), dma((chunks,)), dma((chunks,)), dma((chunks,)),
        ]
        + [pair] * 8
        + [dma((n_dp - 1,)), dma((n_dp - 1,)), pair, pair],
        cost_estimate=pl.CostEstimate(
            flops=rows * (hid + po.shape[1]),
            bytes_accessed=sum(a.size * a.dtype.itemsize for a in args),
            transcendentals=0,
        ),
        compiler_params=pltpu.CompilerParams(
            collective_id=0, has_side_effects=True, vmem_limit_bytes=60 * 1024 * 1024
        ),
    )(*args)


def solution(mesh):
    placed = (
        P("dp", None, "tensor"),
        P("dp", None, "tensor"),
        P("dp", None, "tensor"),
        P("dp", None, "tensor"),
        P(None, "tensor"),
        P(None, "tensor"),
        P(),
        P(),
    )
    body = functools.partial(shards, mesh.shape["dp"], mesh.shape["tensor"])
    return jax.shard_map(
        body, mesh=mesh, in_specs=placed, out_specs=P("dp", "tensor"), check_vma=False
    )
```

```python
import functools
import math

import jax
import jax.numpy as jnp
from jax import lax
from jax.experimental import pallas as pl
from jax.experimental.pallas import tpu as pltpu
from jax.sharding import PartitionSpec as P

MESH = pl.DeviceIdType.MESH


def each(low, high, step):
    if high - low <= 16:
        for k in range(low, high):
            step(k)
    else:
        lax.fori_loop(low, high, lambda k, _: (step(k), 0)[1], 0)


def project(rows, factor):
    return lax.dot_general(
        rows, factor, (((1,), (1,)), ((), ())), preferred_element_type=jnp.float32
    )


def hi_lo(x):
    hi = x.astype(jnp.bfloat16)
    return hi, (x - hi.astype(jnp.float32)).astype(jnp.bfloat16)


def hi_beside_lo(twins):
    hi, lo = hi_lo(twins)
    lane = lax.broadcasted_iota(jnp.int32, twins.shape, 1)
    return jnp.where(lane < twins.shape[1] // 2, hi.astype(jnp.float32), lo.astype(jnp.float32)).astype(
        jnp.bfloat16
    )


def twins(x):
    return jnp.concatenate([x, x], axis=1)


def fold_twins(y):
    width = y.shape[1] // 2
    while width > 64:
        y = y[:, :width] + y[:, width:]
        width //= 2
    return y + jnp.concatenate([y[:, width:], y[:, :width]], axis=1)


def dot(a, b):
    return jnp.dot(a, b, preferred_element_type=jnp.float32)


def fold_rows(y):
    height = y.shape[0] // 2
    return y[:height] + y[height:]


def pack(own, fold):
    rows, lanes = own.shape
    if fold == 1:
        return own[:, : lanes // 2]
    lane = lax.broadcasted_iota(jnp.int32, (rows // 2, lanes), 1)
    return jnp.where(lane < lanes // 2, own[: rows // 2], own[rows // 2 :])


def kernel(
    n_dp, n_tensor, chunks, fold, factor,
    th_hbm, tg_hbm, qh_hbm, qg_hbm, pi_hbm, po_hbm, ci_hbm, co_hbm,
    out_ref,
    th, tg, qh, qg, pi, po, ci, co,
    rq_own, rq_in, rt_own, rt_in, lq_own, lq_in, lt_own, lt_in, gathered, part, part_in,
    load_sem, pi_sem, qh_sem, th_sem,
    rq_send, rq_recv, rt_send, rt_recv, lq_send, lq_recv, lt_send, lt_recv,
    g_send, g_recv, p_send, p_recv,
):
    me_dp = lax.axis_index("dp")
    me_t = lax.axis_index("tensor")
    hid = pi.shape[1]
    step = hid // chunks

    def load(src, dst, sem):
        return pltpu.make_async_copy(src, dst, sem)

    def piece(c):
        return pl.ds(pl.multiple_of(c * step, step), step)

    po_load = load(po_hbm, po, load_sem.at[0])
    qg_load = load(qg_hbm, qg, load_sem.at[1])
    tg_load = load(tg_hbm, tg, load_sem.at[2])
    ci_load = load(ci_hbm, ci, load_sem.at[3])
    co_load = load(co_hbm, co, load_sem.at[4])
    pi_load = lambda c: load(pi_hbm.at[:, piece(c)], pi.at[:, piece(c)], pi_sem.at[c])
    qh_load = lambda c: load(qh_hbm.at[:, :, piece(c)], qh.at[:, :, piece(c)], qh_sem.at[c])
    th_load = lambda c: load(th_hbm.at[:, :, piece(c)], th.at[:, :, piece(c)], th_sem.at[c])

    po_load.start()
    qg_load.start()

    barrier = pltpu.get_barrier_semaphore()

    def greet_tensor(k):
        peer = lax.rem(me_t + k, n_tensor)
        pl.semaphore_signal(barrier, inc=1, device_id={"tensor": peer}, device_id_type=MESH)

    def greet_dp(k):
        peer = lax.rem(me_dp + k, n_dp)
        pl.semaphore_signal(barrier, inc=1, device_id={"dp": peer}, device_id_type=MESH)

    for c in range(chunks):
        pi_load(c).start()
        qh_load(c).start()
    co_load.start()
    ci_load.start()
    each(1, n_tensor, greet_tensor)
    each(1, n_dp, greet_dp)
    def swap(own, landing, send, recv, k, shared):
        peer = lax.rem(me_t + k, n_tensor)
        return pltpu.make_async_remote_copy(
            src_ref=own if shared else own.at[peer],
            dst_ref=landing.at[k - 1],
            send_sem=send.at[k - 1],
            recv_sem=recv.at[k - 1],
            device_id={"tensor": peer},
            device_id_type=MESH,
        )

    rq_swap = lambda k: swap(rq_own, rq_in, rq_send, rq_recv, k, True)
    rt_swap = lambda k: swap(rt_own, rt_in, rt_send, rt_recv, k, True)
    lq_swap = lambda k: swap(lq_own, lq_in, lq_send, lq_recv, k, False)
    lt_swap = lambda k: swap(lt_own, lt_in, lt_send, lt_recv, k, False)

    def spread(k):
        return pltpu.make_async_remote_copy(
            src_ref=gathered.at[me_dp],
            dst_ref=gathered.at[me_dp],
            send_sem=g_send,
            recv_sem=g_recv,
            device_id={"dp": lax.rem(me_dp + k, n_dp)},
            device_id_type=MESH,
        )

    every_other = pltpu.make_async_remote_copy(
        src_ref=gathered.at[pl.ds(0, n_dp - 1)],
        dst_ref=gathered.at[pl.ds(0, n_dp - 1)],
        send_sem=g_send,
        recv_sem=g_recv,
        device_id={"dp": lax.rem(me_dp + 1, n_dp)},
        device_id_type=MESH,
    )

    def summed(own, landing, one_swap):
        total = own
        for k in range(1, n_tensor):
            one_swap(k).wait_recv()
            total = total + landing[k - 1]
        return total

    rank = ci.shape[0]
    rows = rank // n_tensor

    po_load.wait()
    qg_load.wait()
    tg_load.start()
    rq_own[...] = hi_beside_lo(twins(project(qg[0], po[...])))
    def query_chunk(c, total):
        pi_load(c).wait()
        qh_load(c).wait()
        th_load(c).start()
        return total + project(pi[:, piece(c)], qh[0, :, piece(c)])

    left = lax.fori_loop(
        0, chunks, query_chunk, jnp.zeros((rank, qh.shape[1]), jnp.float32)
    )
    ci_load.wait()
    ci_parts = jnp.concatenate(hi_lo(ci[...]), axis=0)
    left = fold_rows(dot(ci_parts, hi_beside_lo(twins(left))))
    left = hi_beside_lo(fold_twins(left))
    for t in range(n_tensor):
        lq_own[t] = left[t * rows : (t + 1) * rows]
    pl.semaphore_wait(barrier, n_dp + n_tensor - 2)
    for k in range(1, n_tensor):
        lq_swap(k).start()
        rq_swap(k).start()

    tg_load.wait()
    rt_own[...] = hi_beside_lo(twins(project(tg[0], po[...])))
    for k in range(1, n_tensor):
        rt_swap(k).start()

    co_load.wait()
    co_parts = hi_beside_lo(twins(co[...]))
    co_parts = jnp.concatenate([co_parts, co_parts], axis=0)
    right = dot(rq_own[...], co_parts)
    for k in range(1, n_tensor):
        rq_swap(k).wait_recv()
        right = right + dot(rq_in[k - 1], co_parts)
    right = hi_beside_lo(fold_twins(right))
    right = jnp.concatenate([right] * (2 * n_tensor), axis=0)

    def example_chunk(c, total):
        th_load(c).wait()
        return total + project(pi[:, piece(c)], th[0, :, piece(c)])

    before = chunks // 2
    example = lax.fori_loop(
        0, before, example_chunk, jnp.zeros((rank, th.shape[1]), jnp.float32)
    )

    lefts = [lq_own[me_t]]
    for k in range(1, n_tensor):
        lq_swap(k).wait_recv()
        lefts.append(lq_in[k - 1])
    conditioned = fold_twins(dot(jnp.concatenate(lefts, axis=1), right))
    gathered[me_dp] = pack(conditioned, fold).astype(gathered.dtype)
    each(1, n_dp, lambda k: spread(k).start())

    example = lax.fori_loop(before, chunks, example_chunk, example)
    for t in range(n_tensor):
        lt_own[t] = example[t * rows : (t + 1) * rows]
    for k in range(1, n_tensor):
        lt_swap(k).start()

    rights = [rt_own[...]]
    for k in range(1, n_tensor):
        rt_swap(k).wait_recv()
        rights.append(rt_in[k - 1])
    rights = jnp.concatenate(rights, axis=1)
    mine = jnp.concatenate(hi_lo(summed(lt_own[me_t], lt_in, lt_swap)), axis=0)
    share = pack(fold_twins(fold_rows(dot(mine, rights))), fold)

    every_other.wait_recv()
    lanes = jnp.sum(gathered[...].astype(jnp.float32) * share[None], axis=1)
    part[...] = lanes.reshape(part.shape)
    p_swap = lambda k: swap(part, part_in, p_send, p_recv, k, False)
    for k in range(1, n_tensor):
        p_swap(k).start()
    total = summed(part[me_t], part_in, p_swap)
    out_ref[...] = jnp.sum(total.T, axis=0, keepdims=True) * factor

    for one_swap in (rq_swap, rt_swap, lq_swap, lt_swap, p_swap):
        for k in range(1, n_tensor):
            one_swap(k).wait_send()
    every_other.wait_send()


def shards(n_dp, n_tensor, th, tg, qh, qg, pi, po, ci, co):
    rank, hid = pi.shape
    seq, qry = th.shape[1], qh.shape[1]
    share = rank // n_tensor
    fold = 2 if share % 32 == 0 else 1
    packed = (share // fold, rank * fold)
    kept = n_dp // n_tensor
    chunks = 4
    f32, bf16 = jnp.float32, jnp.bfloat16
    dma = pltpu.SemaphoreType.DMA
    others = n_tensor - 1
    factor = 1.0 / (rank * math.sqrt(seq * qry))
    args = (th, tg, qh, qg, pi, po, ci, co)
    pair = dma((others,))
    rows = (seq + qry) * rank * 2
    return pl.pallas_call(
        functools.partial(kernel, n_dp, n_tensor, chunks, fold, factor),
        out_shape=jax.ShapeDtypeStruct((1, kept), f32),
        in_specs=[pl.BlockSpec(memory_space=pltpu.HBM)] * len(args),
        out_specs=pl.BlockSpec(memory_space=pltpu.VMEM),
        scratch_shapes=[pltpu.VMEM(a.shape, a.dtype) for a in args]
        + [
            pltpu.VMEM((qry, 2 * rank), bf16),
            pltpu.VMEM((others, qry, 2 * rank), bf16),
            pltpu.VMEM((seq, 2 * rank), bf16),
            pltpu.VMEM((others, seq, 2 * rank), bf16),
            pltpu.VMEM((n_tensor, share, 2 * rank), bf16),
            pltpu.VMEM((others, share, 2 * rank), bf16),
            pltpu.VMEM((n_tensor, share, seq), f32),
            pltpu.VMEM((others, share, seq), f32),
            pltpu.VMEM((n_dp,) + packed, bf16),
            pltpu.VMEM((n_tensor, kept, packed[1]), f32),
            pltpu.VMEM((others, kept, packed[1]), f32),
            dma((5,)), dma((chunks,)), dma((chunks,)), dma((chunks,)),
        ]
        + [pair] * 8
        + [dma, dma, pair, pair],
        cost_estimate=pl.CostEstimate(
            flops=rows * (hid + po.shape[1]),
            bytes_accessed=sum(a.size * a.dtype.itemsize for a in args),
            transcendentals=0,
        ),
        compiler_params=pltpu.CompilerParams(
            collective_id=0, has_side_effects=True, vmem_limit_bytes=60 * 1024 * 1024
        ),
    )(*args)


def solution(mesh):
    placed = (
        P("dp", None, "tensor"),
        P("dp", None, "tensor"),
        P("dp", None, "tensor"),
        P("dp", None, "tensor"),
        P(None, "tensor"),
        P(None, "tensor"),
        P(),
        P(),
    )
    body = functools.partial(shards, mesh.shape["dp"], mesh.shape["tensor"])
    return jax.shard_map(
        body, mesh=mesh, in_specs=placed, out_specs=P("dp", "tensor"), check_vma=False
    )
```

```python
import functools
import math

import jax
import jax.numpy as jnp
from jax import lax
from jax.experimental import pallas as pl
from jax.experimental.pallas import tpu as pltpu
from jax.sharding import PartitionSpec as P

MESH = pl.DeviceIdType.MESH


def each(low, high, step):
    if high - low <= 16:
        for k in range(low, high):
            step(k)
    else:
        lax.fori_loop(low, high, lambda k, _: (step(k), 0)[1], 0)


def project(rows, factor):
    return lax.dot_general(
        rows, factor, (((1,), (1,)), ((), ())), preferred_element_type=jnp.float32
    )


def hi_lo(x):
    hi = x.astype(jnp.bfloat16)
    return hi, (x - hi.astype(jnp.float32)).astype(jnp.bfloat16)


def hi_beside_lo(twins):
    hi, lo = hi_lo(twins)
    lane = lax.broadcasted_iota(jnp.int32, twins.shape, 1)
    return jnp.where(lane < twins.shape[1] // 2, hi.astype(jnp.float32), lo.astype(jnp.float32)).astype(
        jnp.bfloat16
    )


def twins(x):
    return jnp.concatenate([x, x], axis=1)


def fold_twins(y):
    width = y.shape[1] // 2
    while width > 64:
        y = y[:, :width] + y[:, width:]
        width //= 2
    return y + jnp.concatenate([y[:, width:], y[:, :width]], axis=1)


def dot(a, b):
    return jnp.dot(a, b, preferred_element_type=jnp.float32)


def fold_rows(y):
    height = y.shape[0] // 2
    return y[:height] + y[height:]


def pack(own, fold):
    rows, lanes = own.shape
    if fold == 1:
        return own[:, : lanes // 2]
    lane = lax.broadcasted_iota(jnp.int32, (rows // 2, lanes), 1)
    return jnp.where(lane < lanes // 2, own[: rows // 2], own[rows // 2 :])


def kernel(
    n_dp, n_tensor, chunks, fold, factor,
    th_hbm, tg_hbm, qh_hbm, qg_hbm, pi_hbm, po_hbm, ci_hbm, co_hbm,
    out_ref,
    th, tg, qh, qg, pi, po, ci, co,
    rq_own, rq_in, rt_own, rt_in, lq_own, lq_in, lt_own, lt_in, share_own, share_in, gathered, part, part_in,
    load_sem, pi_sem, qh_sem, th_sem,
    rq_send, rq_recv, rt_send, rt_recv, lq_send, lq_recv, lt_send, lt_recv,
    g_send, g_recv, m_send, m_recv, p_send, p_recv,
):
    me_dp = lax.axis_index("dp")
    me_t = lax.axis_index("tensor")
    n_chip = n_dp // 2
    me_chip, me_core = me_dp // 2, lax.rem(me_dp, 2)
    mate = me_chip * 2 + 1 - me_core
    hid = pi.shape[1]
    step = hid // chunks

    def load(src, dst, sem):
        return pltpu.make_async_copy(src, dst, sem)

    def piece(c):
        return pl.ds(pl.multiple_of(c * step, step), step)

    po_load = load(po_hbm, po, load_sem.at[0])
    qg_load = load(qg_hbm, qg, load_sem.at[1])
    tg_load = load(tg_hbm, tg, load_sem.at[2])
    ci_load = load(ci_hbm, ci, load_sem.at[3])
    co_load = load(co_hbm, co, load_sem.at[4])
    pi_load = lambda c: load(pi_hbm.at[:, piece(c)], pi.at[:, piece(c)], pi_sem.at[c])
    qh_load = lambda c: load(qh_hbm.at[:, :, piece(c)], qh.at[:, :, piece(c)], qh_sem.at[c])
    th_load = lambda c: load(th_hbm.at[:, :, piece(c)], th.at[:, :, piece(c)], th_sem.at[c])

    po_load.start()
    qg_load.start()

    barrier = pltpu.get_barrier_semaphore()

    def greet(dp, tensor):
        pl.semaphore_signal(
            barrier, inc=1, device_id={"dp": dp, "tensor": tensor}, device_id_type=MESH
        )

    def chip(k):
        return lax.rem(me_chip + k, n_chip) * 2 + me_core

    def group(k):
        return lax.rem(me_t + k, n_tensor)

    for c in range(chunks):
        pi_load(c).start()
        qh_load(c).start()
    co_load.start()
    ci_load.start()
    for k in range(1, n_tensor):
        greet(me_dp, group(k))
    for k in range(n_tensor):
        greet(mate, group(k))
    each(1, n_chip, lambda k: greet(chip(k), me_t))
    def swap(own, landing, send, recv, k, shared):
        peer = lax.rem(me_t + k, n_tensor)
        return pltpu.make_async_remote_copy(
            src_ref=own if shared else own.at[peer],
            dst_ref=landing.at[k - 1],
            send_sem=send.at[k - 1],
            recv_sem=recv.at[k - 1],
            device_id={"tensor": peer},
            device_id_type=MESH,
        )

    rq_swap = lambda k: swap(rq_own, rq_in, rq_send, rq_recv, k, True)
    rt_swap = lambda k: swap(rt_own, rt_in, rt_send, rt_recv, k, True)
    lq_swap = lambda k: swap(lq_own, lq_in, lq_send, lq_recv, k, False)
    lt_swap = lambda k: swap(lt_own, lt_in, lt_send, lt_recv, k, False)

    def spread(k):
        return pltpu.make_async_remote_copy(
            src_ref=gathered.at[me_chip],
            dst_ref=gathered.at[me_chip],
            send_sem=g_send,
            recv_sem=g_recv,
            device_id={"dp": chip(k)},
            device_id_type=MESH,
        )

    every_other = pltpu.make_async_remote_copy(
        src_ref=gathered.at[pl.ds(0, n_chip - 1)],
        dst_ref=gathered.at[pl.ds(0, n_chip - 1)],
        send_sem=g_send,
        recv_sem=g_recv,
        device_id={"dp": chip(1)},
        device_id_type=MESH,
    )

    to_mate = pltpu.make_async_remote_copy(
        src_ref=share_own,
        dst_ref=share_in,
        send_sem=m_send,
        recv_sem=m_recv,
        device_id={"dp": mate},
        device_id_type=MESH,
    )

    def hand_over(over, k):
        return pltpu.make_async_remote_copy(
            src_ref=part.at[over, group(k)],
            dst_ref=part_in.at[over, k],
            send_sem=p_send.at[over, k],
            recv_sem=p_recv.at[over, k],
            device_id={"dp": mate if over else me_dp, "tensor": group(k)},
            device_id_type=MESH,
        )

    def summed(own, landing, one_swap):
        total = own
        for k in range(1, n_tensor):
            one_swap(k).wait_recv()
            total = total + landing[k - 1]
        return total

    rank = ci.shape[0]
    rows = rank // n_tensor

    po_load.wait()
    qg_load.wait()
    tg_load.start()
    rq_own[...] = hi_beside_lo(twins(project(qg[0], po[...])))
    def query_chunk(c, total):
        pi_load(c).wait()
        qh_load(c).wait()
        th_load(c).start()
        return total + project(pi[:, piece(c)], qh[0, :, piece(c)])

    left = lax.fori_loop(
        0, chunks, query_chunk, jnp.zeros((rank, qh.shape[1]), jnp.float32)
    )
    ci_load.wait()
    ci_parts = jnp.concatenate(hi_lo(ci[...]), axis=0)
    left = fold_rows(dot(ci_parts, hi_beside_lo(twins(left))))
    left = hi_beside_lo(fold_twins(left))
    for t in range(n_tensor):
        lq_own[t] = left[t * rows : (t + 1) * rows]
    pl.semaphore_wait(barrier, n_chip + 2 * n_tensor - 2)
    for k in range(1, n_tensor):
        lq_swap(k).start()
        rq_swap(k).start()

    tg_load.wait()
    rt_own[...] = hi_beside_lo(twins(project(tg[0], po[...])))
    for k in range(1, n_tensor):
        rt_swap(k).start()

    co_load.wait()
    co_parts = hi_beside_lo(twins(co[...]))
    co_parts = jnp.concatenate([co_parts, co_parts], axis=0)
    right = dot(rq_own[...], co_parts)
    for k in range(1, n_tensor):
        rq_swap(k).wait_recv()
        right = right + dot(rq_in[k - 1], co_parts)
    right = hi_beside_lo(fold_twins(right))
    right = jnp.concatenate([right] * (2 * n_tensor), axis=0)

    def example_chunk(c, total):
        th_load(c).wait()
        return total + project(pi[:, piece(c)], th[0, :, piece(c)])

    before = chunks // 2
    example = lax.fori_loop(
        0, before, example_chunk, jnp.zeros((rank, th.shape[1]), jnp.float32)
    )

    lefts = [lq_own[me_t]]
    for k in range(1, n_tensor):
        lq_swap(k).wait_recv()
        lefts.append(lq_in[k - 1])
    conditioned = fold_twins(dot(jnp.concatenate(lefts, axis=1), right))
    gathered[me_chip] = pack(conditioned, fold).astype(gathered.dtype)
    each(1, n_chip, lambda k: spread(k).start())

    example = lax.fori_loop(before, chunks, example_chunk, example)
    for t in range(n_tensor):
        lt_own[t] = example[t * rows : (t + 1) * rows]
    for k in range(1, n_tensor):
        lt_swap(k).start()

    rights = [rt_own[...]]
    for k in range(1, n_tensor):
        rt_swap(k).wait_recv()
        rights.append(rt_in[k - 1])
    rights = jnp.concatenate(rights, axis=1)
    mine = jnp.concatenate(hi_lo(summed(lt_own[me_t], lt_in, lt_swap)), axis=0)
    share_own[...] = pack(fold_twins(fold_rows(dot(mine, rights))), fold)
    to_mate.start()

    half = part.shape[2]

    def partial_scores(over, share):
        lanes = jnp.sum(gathered[...].astype(jnp.float32) * share[None], axis=1)
        for t in range(n_tensor):
            part[over, t] = lanes[t * half : (t + 1) * half]

    every_other.wait_recv()
    to_mate.wait_recv()
    partial_scores(1, share_in[...])
    for k in range(n_tensor):
        hand_over(1, k).start()
    partial_scores(0, share_own[...])
    for k in range(1, n_tensor):
        hand_over(0, k).start()
    same = part[0, me_t]
    for k in range(1, n_tensor):
        hand_over(0, k).wait_recv()
        same = same + part_in[0, k]
    other = None
    for k in range(n_tensor):
        hand_over(1, k).wait_recv()
        other = part_in[1, k] if other is None else other + part_in[1, k]
    first = jnp.where(me_core == 0, same, other)
    second = jnp.where(me_core == 0, other, same)
    pairs = [x[i : i + 1] for i in range(half) for x in (first, second)]
    total = jnp.concatenate(pairs, axis=0)
    out_ref[...] = jnp.sum(total.T, axis=0, keepdims=True) * factor

    for one_swap in (rq_swap, rt_swap, lq_swap, lt_swap):
        for k in range(1, n_tensor):
            one_swap(k).wait_send()
    every_other.wait_send()
    to_mate.wait_send()
    for over in range(2):
        for k in range(1 - over, n_tensor):
            hand_over(over, k).wait_send()


def shards(n_dp, n_tensor, th, tg, qh, qg, pi, po, ci, co):
    rank, hid = pi.shape
    seq, qry = th.shape[1], qh.shape[1]
    share = rank // n_tensor
    fold = 2 if share % 32 == 0 else 1
    packed = (share // fold, rank * fold)
    kept = n_dp // n_tensor
    chunks = 4
    f32, bf16 = jnp.float32, jnp.bfloat16
    dma = pltpu.SemaphoreType.DMA
    others = n_tensor - 1
    factor = 1.0 / (rank * math.sqrt(seq * qry))
    args = (th, tg, qh, qg, pi, po, ci, co)
    pair = dma((others,))
    rows = (seq + qry) * rank * 2
    return pl.pallas_call(
        functools.partial(kernel, n_dp, n_tensor, chunks, fold, factor),
        out_shape=jax.ShapeDtypeStruct((1, kept), f32),
        in_specs=[pl.BlockSpec(memory_space=pltpu.HBM)] * len(args),
        out_specs=pl.BlockSpec(memory_space=pltpu.VMEM),
        scratch_shapes=[pltpu.VMEM(a.shape, a.dtype) for a in args]
        + [
            pltpu.VMEM((qry, 2 * rank), bf16),
            pltpu.VMEM((others, qry, 2 * rank), bf16),
            pltpu.VMEM((seq, 2 * rank), bf16),
            pltpu.VMEM((others, seq, 2 * rank), bf16),
            pltpu.VMEM((n_tensor, share, 2 * rank), bf16),
            pltpu.VMEM((others, share, 2 * rank), bf16),
            pltpu.VMEM((n_tensor, share, seq), f32),
            pltpu.VMEM((others, share, seq), f32),
            pltpu.VMEM(packed, f32),
            pltpu.VMEM(packed, f32),
            pltpu.VMEM((n_dp // 2,) + packed, bf16),
            pltpu.VMEM((2, n_tensor, kept // 2, packed[1]), f32),
            pltpu.VMEM((2, n_tensor, kept // 2, packed[1]), f32),
            dma((5,)), dma((chunks,)), dma((chunks,)), dma((chunks,)),
        ]
        + [pair] * 8
        + [dma] * 4
        + [dma((2, n_tensor))] * 2,
        cost_estimate=pl.CostEstimate(
            flops=rows * (hid + po.shape[1]),
            bytes_accessed=sum(a.size * a.dtype.itemsize for a in args),
            transcendentals=0,
        ),
        compiler_params=pltpu.CompilerParams(
            collective_id=0, has_side_effects=True, vmem_limit_bytes=60 * 1024 * 1024
        ),
    )(*args)


def solution(mesh):
    placed = (
        P("dp", None, "tensor"),
        P("dp", None, "tensor"),
        P("dp", None, "tensor"),
        P("dp", None, "tensor"),
        P(None, "tensor"),
        P(None, "tensor"),
        P(),
        P(),
    )
    body = functools.partial(shards, mesh.shape["dp"], mesh.shape["tensor"])
    return jax.shard_map(
        body, mesh=mesh, in_specs=placed, out_specs=P("dp", "tensor"), check_vma=False
    )
```

```python
import functools
import math

import jax
import jax.numpy as jnp
from jax import lax
from jax.experimental import pallas as pl
from jax.experimental.pallas import tpu as pltpu
from jax.sharding import PartitionSpec as P

MESH = pl.DeviceIdType.MESH


def each(low, high, step):
    if high - low <= 16:
        for k in range(low, high):
            step(k)
    else:
        lax.fori_loop(low, high, lambda k, _: (step(k), 0)[1], 0)


def project(rows, factor):
    return lax.dot_general(
        rows, factor, (((1,), (1,)), ((), ())), preferred_element_type=jnp.float32
    )


def hi_lo(x):
    hi = x.astype(jnp.bfloat16)
    return hi, (x - hi.astype(jnp.float32)).astype(jnp.bfloat16)


def hi_beside_lo(twins):
    hi, lo = hi_lo(twins)
    lane = lax.broadcasted_iota(jnp.int32, twins.shape, 1)
    return jnp.where(lane < twins.shape[1] // 2, hi.astype(jnp.float32), lo.astype(jnp.float32)).astype(
        jnp.bfloat16
    )


def twins(x):
    return jnp.concatenate([x, x], axis=1)


def fold_twins(y):
    width = y.shape[1] // 2
    while width > 64:
        y = y[:, :width] + y[:, width:]
        width //= 2
    return y + jnp.concatenate([y[:, width:], y[:, :width]], axis=1)


def dot(a, b):
    return jnp.dot(a, b, preferred_element_type=jnp.float32)


def fold_rows(y):
    height = y.shape[0] // 2
    return y[:height] + y[height:]


def pack(own, fold):
    rows, lanes = own.shape
    if fold == 1:
        return own[:, : lanes // 2]
    lane = lax.broadcasted_iota(jnp.int32, (rows // 2, lanes), 1)
    return jnp.where(lane < lanes // 2, own[: rows // 2], own[rows // 2 :])


def kernel(
    n_dp, n_tensor, chunks, fold, factor,
    th_hbm, tg_hbm, qh_hbm, qg_hbm, pi_hbm, po_hbm, ci_hbm, co_hbm,
    out_ref,
    th, tg, qh, qg, pi, po, ci, co,
    rq_own, rq_in, rt_own, rt_in, lq_own, lq_in, lt_own, lt_in, gathered, part, part_in,
    load_sem, pi_sem, qh_sem, th_sem,
    rq_send, rq_recv, rt_send, rt_recv, lq_send, lq_recv, lt_send, lt_recv,
    g_send, g_recv, p_send, p_recv,
):
    me_dp = lax.axis_index("dp")
    me_t = lax.axis_index("tensor")
    hid = pi.shape[1]
    step = hid // chunks

    def load(src, dst, sem):
        return pltpu.make_async_copy(src, dst, sem)

    def piece(c):
        return pl.ds(pl.multiple_of(c * step, step), step)

    po_load = load(po_hbm, po, load_sem.at[0])
    qg_load = load(qg_hbm, qg, load_sem.at[1])
    tg_load = load(tg_hbm, tg, load_sem.at[2])
    ci_load = load(ci_hbm, ci, load_sem.at[3])
    co_load = load(co_hbm, co, load_sem.at[4])
    pi_load = lambda c: load(pi_hbm.at[:, piece(c)], pi.at[:, piece(c)], pi_sem.at[c])
    qh_load = lambda c: load(qh_hbm.at[:, :, piece(c)], qh.at[:, :, piece(c)], qh_sem.at[c])
    th_load = lambda c: load(th_hbm.at[:, :, piece(c)], th.at[:, :, piece(c)], th_sem.at[c])

    po_load.start()
    qg_load.start()

    barrier = pltpu.get_barrier_semaphore()

    def greet_tensor(k):
        peer = lax.rem(me_t + k, n_tensor)
        pl.semaphore_signal(barrier, inc=1, device_id={"tensor": peer}, device_id_type=MESH)

    def greet_dp(k):
        peer = lax.rem(me_dp + k, n_dp)
        pl.semaphore_signal(barrier, inc=1, device_id={"dp": peer}, device_id_type=MESH)

    for c in range(chunks):
        pi_load(c).start()
        qh_load(c).start()
    ci_load.start()
    co_load.start()
    tg_load.start()
    for c in range(chunks):
        th_load(c).start()
    each(1, n_tensor, greet_tensor)
    each(1, n_dp, greet_dp)
    def swap(own, landing, send, recv, k, shared):
        peer = lax.rem(me_t + k, n_tensor)
        return pltpu.make_async_remote_copy(
            src_ref=own if shared else own.at[peer],
            dst_ref=landing.at[k - 1],
            send_sem=send.at[k - 1],
            recv_sem=recv.at[k - 1],
            device_id={"tensor": peer},
            device_id_type=MESH,
        )

    rq_swap = lambda k: swap(rq_own, rq_in, rq_send, rq_recv, k, True)
    rt_swap = lambda k: swap(rt_own, rt_in, rt_send, rt_recv, k, True)
    lq_swap = lambda k: swap(lq_own, lq_in, lq_send, lq_recv, k, False)
    lt_swap = lambda k: swap(lt_own, lt_in, lt_send, lt_recv, k, False)

    def spread(k):
        return pltpu.make_async_remote_copy(
            src_ref=gathered.at[me_dp],
            dst_ref=gathered.at[me_dp],
            send_sem=g_send,
            recv_sem=g_recv,
            device_id={"dp": lax.rem(me_dp + k, n_dp)},
            device_id_type=MESH,
        )

    every_other = pltpu.make_async_remote_copy(
        src_ref=gathered.at[pl.ds(0, n_dp - 1)],
        dst_ref=gathered.at[pl.ds(0, n_dp - 1)],
        send_sem=g_send,
        recv_sem=g_recv,
        device_id={"dp": lax.rem(me_dp + 1, n_dp)},
        device_id_type=MESH,
    )

    def summed(own, landing, one_swap):
        total = own
        for k in range(1, n_tensor):
            one_swap(k).wait_recv()
            total = total + landing[k - 1]
        return total

    rank = ci.shape[0]
    rows = rank // n_tensor

    po_load.wait()
    qg_load.wait()
    rq_own[...] = hi_beside_lo(twins(project(qg[0], po[...])))
    def query_chunk(c, total):
        pi_load(c).wait()
        qh_load(c).wait()
        return total + project(pi[:, piece(c)], qh[0, :, piece(c)])

    left = lax.fori_loop(
        0, chunks, query_chunk, jnp.zeros((rank, qh.shape[1]), jnp.float32)
    )
    ci_load.wait()
    ci_parts = jnp.concatenate(hi_lo(ci[...]), axis=0)
    left = fold_rows(dot(ci_parts, hi_beside_lo(twins(left))))
    left = hi_beside_lo(fold_twins(left))
    for t in range(n_tensor):
        lq_own[t] = left[t * rows : (t + 1) * rows]
    pl.semaphore_wait(barrier, n_dp + n_tensor - 2)
    for k in range(1, n_tensor):
        lq_swap(k).start()
        rq_swap(k).start()

    tg_load.wait()
    rt_own[...] = hi_beside_lo(twins(project(tg[0], po[...])))
    for k in range(1, n_tensor):
        rt_swap(k).start()

    co_load.wait()
    co_parts = hi_beside_lo(twins(co[...]))
    co_parts = jnp.concatenate([co_parts, co_parts], axis=0)
    right = dot(rq_own[...], co_parts)
    for k in range(1, n_tensor):
        rq_swap(k).wait_recv()
        right = right + dot(rq_in[k - 1], co_parts)
    right = hi_beside_lo(fold_twins(right))
    right = jnp.concatenate([right] * (2 * n_tensor), axis=0)

    def example_chunk(c, total):
        th_load(c).wait()
        return total + project(pi[:, piece(c)], th[0, :, piece(c)])

    before = chunks // 2
    example = lax.fori_loop(
        0, before, example_chunk, jnp.zeros((rank, th.shape[1]), jnp.float32)
    )

    lefts = [lq_own[me_t]]
    for k in range(1, n_tensor):
        lq_swap(k).wait_recv()
        lefts.append(lq_in[k - 1])
    conditioned = fold_twins(dot(jnp.concatenate(lefts, axis=1), right))
    gathered[me_dp] = pack(conditioned, fold).astype(gathered.dtype)
    each(1, n_dp, lambda k: spread(k).start())

    example = lax.fori_loop(before, chunks, example_chunk, example)
    for t in range(n_tensor):
        lt_own[t] = example[t * rows : (t + 1) * rows]
    for k in range(1, n_tensor):
        lt_swap(k).start()

    rights = [rt_own[...]]
    for k in range(1, n_tensor):
        rt_swap(k).wait_recv()
        rights.append(rt_in[k - 1])
    rights = jnp.concatenate(rights, axis=1)
    mine = jnp.concatenate(hi_lo(summed(lt_own[me_t], lt_in, lt_swap)), axis=0)
    share = pack(fold_twins(fold_rows(dot(mine, rights))), fold)

    every_other.wait_recv()
    lanes = jnp.sum(gathered[...].astype(jnp.float32) * share[None], axis=1)
    part[...] = lanes.reshape(part.shape)
    p_swap = lambda k: swap(part, part_in, p_send, p_recv, k, False)
    for k in range(1, n_tensor):
        p_swap(k).start()
    total = summed(part[me_t], part_in, p_swap)
    out_ref[...] = jnp.sum(total.T, axis=0, keepdims=True) * factor

    for one_swap in (rq_swap, rt_swap, lq_swap, lt_swap, p_swap):
        for k in range(1, n_tensor):
            one_swap(k).wait_send()
    every_other.wait_send()


def shards(n_dp, n_tensor, th, tg, qh, qg, pi, po, ci, co):
    rank, hid = pi.shape
    seq, qry = th.shape[1], qh.shape[1]
    share = rank // n_tensor
    fold = 2 if share % 32 == 0 else 1
    packed = (share // fold, rank * fold)
    kept = n_dp // n_tensor
    chunks = 4
    f32, bf16 = jnp.float32, jnp.bfloat16
    dma = pltpu.SemaphoreType.DMA
    others = n_tensor - 1
    factor = 1.0 / (rank * math.sqrt(seq * qry))
    args = (th, tg, qh, qg, pi, po, ci, co)
    pair = dma((others,))
    rows = (seq + qry) * rank * 2
    return pl.pallas_call(
        functools.partial(kernel, n_dp, n_tensor, chunks, fold, factor),
        out_shape=jax.ShapeDtypeStruct((1, kept), f32),
        in_specs=[pl.BlockSpec(memory_space=pltpu.HBM)] * len(args),
        out_specs=pl.BlockSpec(memory_space=pltpu.VMEM),
        scratch_shapes=[pltpu.VMEM(a.shape, a.dtype) for a in args]
        + [
            pltpu.VMEM((qry, 2 * rank), bf16),
            pltpu.VMEM((others, qry, 2 * rank), bf16),
            pltpu.VMEM((seq, 2 * rank), bf16),
            pltpu.VMEM((others, seq, 2 * rank), bf16),
            pltpu.VMEM((n_tensor, share, 2 * rank), bf16),
            pltpu.VMEM((others, share, 2 * rank), bf16),
            pltpu.VMEM((n_tensor, share, seq), f32),
            pltpu.VMEM((others, share, seq), f32),
            pltpu.VMEM((n_dp,) + packed, bf16),
            pltpu.VMEM((n_tensor, kept, packed[1]), f32),
            pltpu.VMEM((others, kept, packed[1]), f32),
            dma((5,)), dma((chunks,)), dma((chunks,)), dma((chunks,)),
        ]
        + [pair] * 8
        + [dma, dma, pair, pair],
        cost_estimate=pl.CostEstimate(
            flops=rows * (hid + po.shape[1]),
            bytes_accessed=sum(a.size * a.dtype.itemsize for a in args),
            transcendentals=0,
        ),
        compiler_params=pltpu.CompilerParams(
            collective_id=0, has_side_effects=True, vmem_limit_bytes=60 * 1024 * 1024
        ),
    )(*args)


def solution(mesh):
    placed = (
        P("dp", None, "tensor"),
        P("dp", None, "tensor"),
        P("dp", None, "tensor"),
        P("dp", None, "tensor"),
        P(None, "tensor"),
        P(None, "tensor"),
        P(),
        P(),
    )
    body = functools.partial(shards, mesh.shape["dp"], mesh.shape["tensor"])
    return jax.shard_map(
        body, mesh=mesh, in_specs=placed, out_specs=P("dp", "tensor"), check_vma=False
    )
```

```python
import functools
import math

import jax
import jax.numpy as jnp
from jax import lax
from jax.experimental import pallas as pl
from jax.experimental.pallas import tpu as pltpu
from jax.sharding import PartitionSpec as P

MESH = pl.DeviceIdType.MESH


def each(low, high, step):
    if high - low <= 16:
        for k in range(low, high):
            step(k)
    else:
        lax.fori_loop(low, high, lambda k, _: (step(k), 0)[1], 0)


def project(rows, factor):
    return lax.dot_general(
        rows, factor, (((1,), (1,)), ((), ())), preferred_element_type=jnp.float32
    )


def hi_lo(x):
    hi = x.astype(jnp.bfloat16)
    return hi, (x - hi.astype(jnp.float32)).astype(jnp.bfloat16)


def hi_beside_lo(twins):
    hi, lo = hi_lo(twins)
    lane = lax.broadcasted_iota(jnp.int32, twins.shape, 1)
    return jnp.where(lane < twins.shape[1] // 2, hi.astype(jnp.float32), lo.astype(jnp.float32)).astype(
        jnp.bfloat16
    )


def twins(x):
    return jnp.concatenate([x, x], axis=1)


def fold_twins(y):
    width = y.shape[1] // 2
    while width > 64:
        y = y[:, :width] + y[:, width:]
        width //= 2
    return y + jnp.concatenate([y[:, width:], y[:, :width]], axis=1)


def dot(a, b):
    return jnp.dot(a, b, preferred_element_type=jnp.float32)


def fold_rows(y):
    height = y.shape[0] // 2
    return y[:height] + y[height:]


def pack(own, fold):
    rows, lanes = own.shape
    if fold == 1:
        return own[:, : lanes // 2]
    lane = lax.broadcasted_iota(jnp.int32, (rows // 2, lanes), 1)
    return jnp.where(lane < lanes // 2, own[: rows // 2], own[rows // 2 :])


def kernel(
    n_dp, n_tensor, chunks, fold, factor,
    th_hbm, tg_hbm, qh_hbm, qg_hbm, pi_hbm, po_hbm, ci_hbm, co_hbm,
    out_ref,
    th, tg, qh, qg, pi, po, ci, co,
    rq_own, rq_in, rt_own, rt_in, lq_own, lq_in, lt_own, lt_in, gathered, part, part_in,
    load_sem, pi_sem, qh_sem, th_sem,
    rq_send, rq_recv, rt_send, rt_recv, lq_send, lq_recv, lt_send, lt_recv,
    g_send, g_recv, p_send, p_recv,
):
    me_dp = lax.axis_index("dp")
    me_t = lax.axis_index("tensor")
    hid = pi.shape[1]
    step = hid // chunks

    def load(src, dst, sem):
        return pltpu.make_async_copy(src, dst, sem)

    def piece(c):
        return pl.ds(pl.multiple_of(c * step, step), step)

    po_load = load(po_hbm, po, load_sem.at[0])
    qg_load = load(qg_hbm, qg, load_sem.at[1])
    tg_load = load(tg_hbm, tg, load_sem.at[2])
    ci_load = load(ci_hbm, ci, load_sem.at[3])
    co_load = load(co_hbm, co, load_sem.at[4])
    pi_load = lambda c: load(pi_hbm.at[:, piece(c)], pi.at[:, piece(c)], pi_sem.at[c])
    qh_load = lambda c: load(qh_hbm.at[:, :, piece(c)], qh.at[:, :, piece(c)], qh_sem.at[c])
    th_load = lambda c: load(th_hbm.at[:, :, piece(c)], th.at[:, :, piece(c)], th_sem.at[c])

    po_load.start()
    qg_load.start()

    barrier = pltpu.get_barrier_semaphore()

    def greet_tensor(k):
        peer = lax.rem(me_t + k, n_tensor)
        pl.semaphore_signal(barrier, inc=1, device_id={"tensor": peer}, device_id_type=MESH)

    def greet_dp(k):
        peer = lax.rem(me_dp + k, n_dp)
        pl.semaphore_signal(barrier, inc=1, device_id={"dp": peer}, device_id_type=MESH)

    for c in range(chunks):
        pi_load(c).start()
        qh_load(c).start()
    co_load.start()
    ci_load.start()
    each(1, n_tensor, greet_tensor)
    each(1, n_dp, greet_dp)
    def swap(own, landing, send, recv, k, shared):
        peer = lax.rem(me_t + k, n_tensor)
        return pltpu.make_async_remote_copy(
            src_ref=own if shared else own.at[peer],
            dst_ref=landing.at[k - 1],
            send_sem=send.at[k - 1],
            recv_sem=recv.at[k - 1],
            device_id={"tensor": peer},
            device_id_type=MESH,
        )

    rq_swap = lambda k: swap(rq_own, rq_in, rq_send, rq_recv, k, True)
    rt_swap = lambda k: swap(rt_own, rt_in, rt_send, rt_recv, k, True)
    lq_swap = lambda k: swap(lq_own, lq_in, lq_send, lq_recv, k, False)
    lt_swap = lambda k: swap(lt_own, lt_in, lt_send, lt_recv, k, False)

    def spread(k):
        return pltpu.make_async_remote_copy(
            src_ref=gathered.at[me_dp],
            dst_ref=gathered.at[me_dp],
            send_sem=g_send,
            recv_sem=g_recv,
            device_id={"dp": lax.rem(me_dp + k, n_dp)},
            device_id_type=MESH,
        )

    every_other = pltpu.make_async_remote_copy(
        src_ref=gathered.at[pl.ds(0, n_dp - 1)],
        dst_ref=gathered.at[pl.ds(0, n_dp - 1)],
        send_sem=g_send,
        recv_sem=g_recv,
        device_id={"dp": lax.rem(me_dp + 1, n_dp)},
        device_id_type=MESH,
    )

    def summed(own, landing, one_swap):
        total = own
        for k in range(1, n_tensor):
            one_swap(k).wait_recv()
            total = total + landing[k - 1]
        return total

    rank = ci.shape[0]
    rows = rank // n_tensor

    po_load.wait()
    qg_load.wait()
    tg_load.start()
    rq_own[...] = hi_beside_lo(twins(project(qg[0], po[...])))
    def query_chunk(c, total):
        pi_load(c).wait()
        qh_load(c).wait()
        th_load(c).start()
        return total + project(pi[:, piece(c)], qh[0, :, piece(c)])

    left = lax.fori_loop(
        0, chunks, query_chunk, jnp.zeros((rank, qh.shape[1]), jnp.float32)
    )
    ci_load.wait()
    ci_parts = jnp.concatenate(hi_lo(ci[...]), axis=0)
    left = fold_rows(dot(ci_parts, hi_beside_lo(twins(left))))
    left = hi_beside_lo(fold_twins(left))
    for t in range(n_tensor):
        lq_own[t] = left[t * rows : (t + 1) * rows]
    pl.semaphore_wait(barrier, n_dp + n_tensor - 2)
    for k in range(1, n_tensor):
        lq_swap(k).start()
        rq_swap(k).start()

    tg_load.wait()
    rt_own[...] = hi_beside_lo(twins(project(tg[0], po[...])))
    for k in range(1, n_tensor):
        rt_swap(k).start()

    co_load.wait()
    co_parts = hi_beside_lo(twins(co[...]))
    co_parts = jnp.concatenate([co_parts, co_parts], axis=0)
    right = dot(rq_own[...], co_parts)
    for k in range(1, n_tensor):
        rq_swap(k).wait_recv()
        right = right + dot(rq_in[k - 1], co_parts)
    right = hi_beside_lo(fold_twins(right))
    right = jnp.concatenate([right] * (2 * n_tensor), axis=0)

    def example_chunk(c, total):
        th_load(c).wait()
        return total + project(pi[:, piece(c)], th[0, :, piece(c)])

    before = chunks // 4
    example = lax.fori_loop(
        0, before, example_chunk, jnp.zeros((rank, th.shape[1]), jnp.float32)
    )

    lefts = [lq_own[me_t]]
    for k in range(1, n_tensor):
        lq_swap(k).wait_recv()
        lefts.append(lq_in[k - 1])
    conditioned = fold_twins(dot(jnp.concatenate(lefts, axis=1), right))
    gathered[me_dp] = pack(conditioned, fold).astype(gathered.dtype)
    each(1, n_dp, lambda k: spread(k).start())

    example = lax.fori_loop(before, chunks, example_chunk, example)
    for t in range(n_tensor):
        lt_own[t] = example[t * rows : (t + 1) * rows]
    for k in range(1, n_tensor):
        lt_swap(k).start()

    rights = [rt_own[...]]
    for k in range(1, n_tensor):
        rt_swap(k).wait_recv()
        rights.append(rt_in[k - 1])
    rights = jnp.concatenate(rights, axis=1)
    mine = jnp.concatenate(hi_lo(summed(lt_own[me_t], lt_in, lt_swap)), axis=0)
    share = pack(fold_twins(fold_rows(dot(mine, rights))), fold)

    every_other.wait_recv()
    lanes = jnp.sum(gathered[...].astype(jnp.float32) * share[None], axis=1)
    part[...] = lanes.reshape(part.shape)
    p_swap = lambda k: swap(part, part_in, p_send, p_recv, k, False)
    for k in range(1, n_tensor):
        p_swap(k).start()
    total = summed(part[me_t], part_in, p_swap)
    out_ref[...] = jnp.sum(total.T, axis=0, keepdims=True) * factor

    for one_swap in (rq_swap, rt_swap, lq_swap, lt_swap, p_swap):
        for k in range(1, n_tensor):
            one_swap(k).wait_send()
    every_other.wait_send()


def shards(n_dp, n_tensor, th, tg, qh, qg, pi, po, ci, co):
    rank, hid = pi.shape
    seq, qry = th.shape[1], qh.shape[1]
    share = rank // n_tensor
    fold = 2 if share % 32 == 0 else 1
    packed = (share // fold, rank * fold)
    kept = n_dp // n_tensor
    chunks = 4
    f32, bf16 = jnp.float32, jnp.bfloat16
    dma = pltpu.SemaphoreType.DMA
    others = n_tensor - 1
    factor = 1.0 / (rank * math.sqrt(seq * qry))
    args = (th, tg, qh, qg, pi, po, ci, co)
    pair = dma((others,))
    rows = (seq + qry) * rank * 2
    return pl.pallas_call(
        functools.partial(kernel, n_dp, n_tensor, chunks, fold, factor),
        out_shape=jax.ShapeDtypeStruct((1, kept), f32),
        in_specs=[pl.BlockSpec(memory_space=pltpu.HBM)] * len(args),
        out_specs=pl.BlockSpec(memory_space=pltpu.VMEM),
        scratch_shapes=[pltpu.VMEM(a.shape, a.dtype) for a in args]
        + [
            pltpu.VMEM((qry, 2 * rank), bf16),
            pltpu.VMEM((others, qry, 2 * rank), bf16),
            pltpu.VMEM((seq, 2 * rank), bf16),
            pltpu.VMEM((others, seq, 2 * rank), bf16),
            pltpu.VMEM((n_tensor, share, 2 * rank), bf16),
            pltpu.VMEM((others, share, 2 * rank), bf16),
            pltpu.VMEM((n_tensor, share, seq), f32),
            pltpu.VMEM((others, share, seq), f32),
            pltpu.VMEM((n_dp,) + packed, bf16),
            pltpu.VMEM((n_tensor, kept, packed[1]), f32),
            pltpu.VMEM((others, kept, packed[1]), f32),
            dma((5,)), dma((chunks,)), dma((chunks,)), dma((chunks,)),
        ]
        + [pair] * 8
        + [dma, dma, pair, pair],
        cost_estimate=pl.CostEstimate(
            flops=rows * (hid + po.shape[1]),
            bytes_accessed=sum(a.size * a.dtype.itemsize for a in args),
            transcendentals=0,
        ),
        compiler_params=pltpu.CompilerParams(
            collective_id=0, has_side_effects=True, vmem_limit_bytes=60 * 1024 * 1024
        ),
    )(*args)


def solution(mesh):
    placed = (
        P("dp", None, "tensor"),
        P("dp", None, "tensor"),
        P("dp", None, "tensor"),
        P("dp", None, "tensor"),
        P(None, "tensor"),
        P(None, "tensor"),
        P(),
        P(),
    )
    body = functools.partial(shards, mesh.shape["dp"], mesh.shape["tensor"])
    return jax.shard_map(
        body, mesh=mesh, in_specs=placed, out_specs=P("dp", "tensor"), check_vma=False
    )
```
